1024 devices in a mesh: dp: 64 (over x, z), fsdp: 16 (over y, core).
Axes of the slice: x: 8, y: 8, z: 8, core: 2. Of those that a mesh axis runs over, the one named last changes fastest.
Arguments:
- attn: bfloat16 [64, 2, 1024, 4096], P('dp', None, 'fsdp')
- resid: bfloat16 [64, 2, 1024, 4096], P('dp', None, 'fsdp')
- lengths: int32 [64, 2], P('dp'), may hold values from 1 to 1024, as said below
- out_proj: bfloat16 [4096, 4096], P('fsdp'), may hold values from -0.09375 to 0.09375
- norm_gain: float32 [4096], replicated, may hold values from 0.5 to 1.5
- bank: bfloat16 [128, 4096], P('dp'), may hold values from -6 to 6
- hard_ids: int32 [64, 8], replicated, may hold values from 0 to 127
Outputs:
- loss: float32 [], replicated
- grad_out_proj: float32 [4096, 4096], P('dp', 'fsdp')
The draws below stay inside these ranges and needn't reach their ends.
Inputs may be any that keep to these rules, and one draw needn't show every extreme that they name: The pooled position of a sequence is its last one, lengths - 1.
All inputs are finite; a program needn't handle non-finite values.
Results may differ from the reference program's by a relative error of at most 0.0052.
Values may be sent and summed in bfloat16 or wider, within the bound.
A program may use at most 32 MiB of HBM per device.

```python
import math
import jax
import jax.numpy as jnp
import numpy as np
from jax import lax

D = 4096
LEN = 1024
HN = 8
S = 64
NB = 128


def pair_states(key):
    base_key = jax.random.fold_in(key, 0)
    base = jax.random.normal(base_key, (S, 2, LEN, D), jnp.float32)
    return base.astype(jnp.bfloat16)


def draw_attn(key, part):
    key = jax.random.fold_in(key, 11)
    return pair_states(key)


def draw_resid(key, part):
    key = jax.random.fold_in(key, 23)
    return pair_states(key)


def draw_lengths(key, part):
    key = jax.random.fold_in(key, 37)
    first_key, second_key, spot_key = jax.random.split(key, 3)
    first = jax.random.randint(first_key, (S, 2), 1, LEN + 1, dtype=jnp.int32)
    second = jax.random.randint(second_key, (S, 2), 1, LEN + 1, dtype=jnp.int32)
    spread = jnp.minimum(first, second)
    spot = jax.random.randint(spot_key, (), 0, S, dtype=jnp.int32)
    return spread.at[spot, 1].set(LEN)


def place_ends(result, rng, smallest, largest):
    place = [jax.random.randint(jax.random.fold_in(rng, axis), (), 0, length) for axis, length in enumerate(result.shape)]
    main_axis = result.shape.index(max(result.shape))
    beside = place[:main_axis] + [(place[main_axis] + 1) % result.shape[main_axis]] + place[main_axis + 1:]
    return result.at[tuple(place)].set(smallest).at[tuple(beside)].set(largest)


def level_of(stream_key, dims, shards, low, high):
    gain = 1.0
    for axis_at, parts in shards:
        draws = jax.random.uniform(jax.random.fold_in(jax.random.fold_in(stream_key, 6), axis_at), (parts,), jnp.float32, low / len(shards), high / len(shards))
        gain = gain * jnp.repeat(jnp.exp(draws), dims[axis_at] // parts).reshape((-1,) + (1,) * (len(dims) - 1 - axis_at))
    return gain


def cumulative_ranks(count, lean):
    loads = [(1 << 20) // math.isqrt(rank ** lean) + 1 for rank in range(1, count + 1)]
    deviation = 1 + sum(loads) // (1 << 30)
    return np.cumsum(np.array([max(1, weight // deviation) for weight in loads]))


def skewed_ids(rng, shape, number_of, lean):
    table = cumulative_ranks(number_of, lean)
    ticket = jax.random.randint(jax.random.fold_in(rng, 1), shape, 0, int(table[number_of - 1]))
    standing = jnp.searchsorted(jnp.asarray(table, jnp.int32), ticket, side="right")
    return jax.random.permutation(jax.random.fold_in(rng, 2), number_of)[standing].astype(jnp.int32)


def normal_values(rng, extent, width, limit, pieces=(), kind=jnp.bfloat16):
    result = jax.random.normal(rng, extent, jnp.float32) * width
    if len(pieces) > 0:
        result = level_of(rng, extent, pieces, -0.22, 0.18) * result
    return jnp.clip(result, min=-limit, max=limit).astype(kind)


def setup_inputs(seed: int = 0) -> dict:
    keys = jax.random.split(jax.random.key(seed), 8)
    return {
        "attn": draw_attn(jax.random.fold_in(keys[7], 71), 0),
        "resid": draw_resid(jax.random.fold_in(keys[7], 71), 0),
        "lengths": draw_lengths(jax.random.fold_in(keys[7], 71), 0),
        "out_proj": normal_values(keys[3], (D, D), D ** -0.5, 0.09375, ((0, 16),)),
        "norm_gain": jnp.clip(1.0 + 0.1 * jax.random.normal(keys[4], (D,), jnp.float32), 0.5, 1.5),
        "bank": normal_values(keys[5], (NB, D), 1.0, 6.0, ((0, 64),)),
        "hard_ids": place_ends(skewed_ids(keys[6], (S, HN), NB, 2), jax.random.fold_in(keys[6], 3), 0, NB - 1).astype(jnp.int32),
    }


def reference(attn, resid, lengths, out_proj, norm_gain, bank, hard_ids):
    places = (lengths - 1).astype(jnp.int32)[:, :, None, None]
    pooled_attn = jnp.take_along_axis(attn, places, axis=2)[:, :, 0]
    pooled_resid = jnp.take_along_axis(resid, places, axis=2)[:, :, 0]
    attn_rows = pooled_attn.reshape(2 * S, D)
    hidden = pooled_resid.reshape(2 * S, D).astype(jnp.float32) + jnp.dot(attn_rows, out_proj, preferred_element_type=jnp.float32)
    inv_rms = lax.rsqrt(lax.optimization_barrier(jnp.mean(hidden * hidden, axis=-1, keepdims=True)) + 1e-05)
    normed = hidden * inv_rms
    emb = (normed * norm_gain).astype(jnp.bfloat16).reshape(S, 2, D)
    queries = emb[:, 0]
    passages = emb[:, 1]
    scale = 4.0 / D ** 0.5
    scores = jnp.dot(queries, passages.T, preferred_element_type=jnp.float32) * scale
    chosen = bank[hard_ids].astype(jnp.float32)
    hard = jnp.einsum('sd,shd->sh', queries.astype(jnp.float32), chosen, precision=lax.Precision.HIGHEST) * scale
    row_lse = jax.nn.logsumexp(jnp.concatenate([scores, hard], axis=1), axis=1)
    col_lse = jax.nn.logsumexp(scores, axis=0)
    diag = jnp.diagonal(scores)
    loss = (jnp.sum(row_lse - diag) + jnp.sum(col_lse - diag)) / (2.0 * S)
    eye = jnp.eye(S, dtype=jnp.float32)
    dscore = (jnp.exp(scores - row_lse[:, None]) + jnp.exp(scores - col_lse[None, :]) - 2.0 * eye) / (2.0 * S)
    dhard = jnp.exp(hard - row_lse[:, None]) / (2.0 * S)
    grad_query = jnp.dot(dscore, passages.astype(jnp.float32), precision=lax.Precision.HIGHEST)
    grad_query = (grad_query + jnp.einsum('sh,shd->sd', dhard, chosen, precision=lax.Precision.HIGHEST)) * scale
    grad_passage = jnp.dot(dscore.T, queries.astype(jnp.float32), precision=lax.Precision.HIGHEST) * scale
    grad_emb = jnp.stack([grad_query, grad_passage], axis=1).reshape(2 * S, D)
    dz = grad_emb * norm_gain
    centre = lax.optimization_barrier(jnp.mean(normed * dz, axis=-1, keepdims=True))
    grad_hidden = inv_rms * (dz - normed * centre)
    grad_out_proj = jnp.dot(attn_rows.astype(jnp.float32).T, grad_hidden, precision=lax.Precision.HIGHEST)
    return (loss, grad_out_proj)
```

```python
import jax
import jax.numpy as jnp
from jax import lax
from jax.experimental import pallas as pl
from jax.experimental.pallas import tpu as pltpu
from jax.sharding import PartitionSpec as P

MESH = pl.DeviceIdType.MESH
F32 = jnp.float32
BF16 = jnp.bfloat16

SIDE = 8
DP = 64
FS = 16
D = 4096
BLK = 256
SCALE = 4.0 / 64.0
COUNT = 128.0

ATTN, RESID, BANK, COLS, PAIR, YSUM, SQ, NORM, INV, RELAY, SPAIR, SY, SBACK = range(13)
KINDS = 13


def far(m):
    return lax.rem(12 + (2 * lax.rem(m, 2) - 1) * lax.div(m + 1, 2), SIDE)


def dot(a, b, ca, cb):
    return lax.dot_general(a, b, (((ca,), (cb,)), ((), ())), preferred_element_type=F32)


def dot2(a, b, ca, cb):
    hi = a.astype(BF16)
    lo = (a - hi.astype(F32)).astype(BF16)
    return dot(hi, b, ca, cb) + dot(lo, b, ca, cb)


def kernel(
    attn, resid, lengths, w, gain, bank, ids, loss_out, grad_out,
    attn_v, resid_v, len_s, w_v, gain_v, bank_v, ids_v,
    src1, rcv1, lhs, part, cbuf, half, ybuf, hid, sq, sqr,
    nsrc, nbuf, isrc, ibuf, bsrc, bbuf, asrc, abuf, at_full, at_buf,
    pay, cb4, half4, yb4, tot, flat, local_sem, ssem, rsem,
):
    i = lax.axis_index("dp")
    j = lax.axis_index("fsdp")
    x, z = lax.div(i, SIDE), lax.rem(i, SIDE)
    y, c = lax.div(j, 2), lax.rem(j, 2)
    partner = (i, 2 * y + 1 - c)

    def dp_peer(t):
        px = lax.rem(x + far(lax.div(t, SIDE)), SIDE)
        pz = lax.rem(z + far(lax.rem(t, SIDE)), SIDE)
        return (px * SIDE + pz, j)

    def fs_index(t):
        return 2 * lax.rem(y + far(lax.div(t, 2)), SIDE) + lax.rem(c + t + 1, 2)

    def y_peer(t):
        return (i, 2 * lax.rem(y + far(t), SIDE) + c)

    def send(src, dst, kind, to):
        pltpu.make_async_remote_copy(
            src_ref=src, dst_ref=dst, send_sem=ssem.at[kind], recv_sem=rsem.at[kind],
            device_id=to, device_id_type=MESH,
        ).start()

    def arrived(ref, kind):
        pltpu.make_async_copy(ref, ref, rsem.at[kind]).wait()

    def sent(ref, kind):
        pltpu.make_async_copy(ref, ref, ssem.at[kind]).wait()

    loads = [
        pltpu.make_async_copy(a, b, local_sem.at[n])
        for n, (a, b) in enumerate([
            (lengths, len_s), (attn.at[0], attn_v), (resid.at[0], resid_v), (bank, bank_v),
            (ids, ids_v), (gain, gain_v), (w, w_v),
        ])
    ]
    for load in loads:
        load.start()

    barrier = pltpu.get_barrier_semaphore()

    @pl.loop(0, DP - 1)
    def _(t):
        pl.semaphore_signal(barrier, inc=1, device_id=dp_peer(t), device_id_type=MESH)

    @pl.loop(0, FS - 1)
    def _(t):
        pl.semaphore_signal(barrier, inc=1, device_id=(i, fs_index(t)), device_id_type=MESH)

    loads[0].wait()
    loads[1].wait()
    row = lax.broadcasted_iota(jnp.int32, (16, 128), 0)
    col = lax.broadcasted_iota(jnp.int32, (16, 128), 1)
    place_q = len_s[0, 0] - 1 - 64 * j
    place_p = len_s[0, 1] - 1 - 64 * j
    pick = jnp.where(
        row < 2,
        jnp.where(col < 64, col, -1) - place_q,
        jnp.where(col >= 64, col - 64, -1) - place_p,
    )
    inside = jnp.where(row < 2, jnp.where(col < 64, 1, 0), jnp.where(col >= 64, 1, 0))
    select = jnp.where((pick == 0) & (inside == 1), 1.0, 0.0).astype(BF16)
    even = lax.rem(row, 2) == 0

    def fold(block):
        return jnp.where(even, block[:, :128], block[:, 128:])[0:4]

    for t in range(FS):
        src1[0, t] = fold(dot(select, attn_v[:, :, t * BLK:(t + 1) * BLK].reshape(128, BLK), 1, 0))
    rcv1[0, j] = src1[0, j]
    pl.semaphore_wait(barrier, DP - 1 + FS - 1)

    @pl.loop(0, FS - 1)
    def _(t):
        to = fs_index(t)
        send(src1.at[0, to], rcv1.at[0, j], ATTN, (i, to))

    loads[2].wait()
    for t in range(FS):
        src1[1, t] = fold(dot(select, resid_v[:, :, t * BLK:(t + 1) * BLK].reshape(128, BLK), 1, 0))
    rcv1[1, j] = src1[1, j]

    @pl.loop(0, FS - 1)
    def _(t):
        to = fs_index(t)
        send(src1.at[1, to], rcv1.at[1, j], RESID, (i, to))

    loads[3].wait()
    own = pl.ds(pl.multiple_of(j * BLK, BLK), BLK)
    bank_rows = bank_v[:, own].astype(F32)
    bsrc[0:1] = bank_rows[0:1, :128]
    bsrc[1:2] = bank_rows[0:1, 128:]
    bsrc[2:3] = bank_rows[1:2, :128]
    bsrc[3:4] = bank_rows[1:2, 128:]
    bbuf[i] = bsrc[...]

    @pl.loop(0, DP - 1)
    def _(t):
        send(bsrc, bbuf.at[i], BANK, dp_peer(t))

    lhs[...] = jnp.zeros_like(lhs)
    loads[6].wait()

    arrived(rcv1.at[0, pl.ds(0, FS - 1)], ATTN)
    block = jnp.sum(rcv1[0], axis=0)
    asrc[...] = block
    for r in range(4):
        lhs[r:r + 1, 0:128] = block[r - r % 2:r - r % 2 + 1]
        lhs[r:r + 1, 128:256] = block[r - r % 2 + 1:r - r % 2 + 2]
    rows = lhs[...].astype(BF16)
    for t in range(FS):
        part[t % 2, t // 2] = fold(dot(rows, w_v[:, t * BLK:(t + 1) * BLK], 1, 0))
    arrived(rcv1.at[1, pl.ds(0, FS - 1)], RESID)
    part[c, y] = part[c, y] + jnp.sum(rcv1[1], axis=0)
    send(part.at[1 - c], cbuf, PAIR, partner)

    @pl.loop(0, 4)
    def _(t):
        to = 4 * j + t

        @pl.when(to != i)
        def _():
            send(asrc, abuf.at[i], COLS, (to, j))

    relay = lax.div(i, 4)

    @pl.when(relay == j)
    def _():
        abuf[i] = asrc[...]

    arrived(cbuf, PAIR)
    half[...] = part[c] + cbuf[...]
    ybuf[y] = half[...]

    @pl.loop(0, SIDE - 1)
    def _(t):
        send(half, ybuf.at[y], YSUM, y_peer(t))

    loads[4].wait()
    loads[5].wait()
    eye = lax.broadcasted_iota(jnp.int32, (64, 64), 0) == lax.broadcasted_iota(jnp.int32, (64, 64), 1)
    eye_f = jnp.where(eye, 1.0, 0.0)
    ids_t = ids_v[...]
    spot = lax.rem(ids_t, 2) * 64 + lax.div(ids_t, 2)
    bank_row = lax.broadcasted_iota(jnp.int32, (128, 64), 0)

    arrived(ybuf.at[pl.ds(0, SIDE - 1)], YSUM)
    hid[...] = jnp.sum(ybuf[...], axis=0)
    sq[...] = jnp.sum(hid[...] * hid[...], axis=0)
    send(sq, sqr, SQ, partner)
    arrived(sqr, SQ)
    sums = jnp.sum(sq[...] + sqr[...], axis=1, keepdims=True)
    inv_q = lax.rsqrt((sums[0:1] + sums[1:2]) * (1.0 / D) + 1e-5)
    inv_p = lax.rsqrt((sums[2:3] + sums[3:4]) * (1.0 / D) + 1e-5)
    four = lax.broadcasted_iota(jnp.int32, (4, 128), 0)
    nsrc[...] = hid[y] * jnp.where(four < 2, inv_q, inv_p)
    lane = lax.broadcasted_iota(jnp.int32, (1, 128), 1)
    isrc[...] = jnp.where(lane < 64, inv_q, inv_p)

    @pl.loop(0, DP - 1)
    def _(t):
        send(nsrc, nbuf.at[i], NORM, dp_peer(t))

    nbuf[i] = nsrc[...]
    ibuf[i] = isrc[...]

    @pl.loop(0, DP - 1)
    def _(t):
        send(isrc, ibuf.at[i], INV, dp_peer(t))

    @pl.when(relay == j)
    def _():
        arrived(abuf.at[pl.ds(0, DP - 1)], COLS)
        low = lax.rem(i, 4) < 2
        rows_q = jnp.where(low, abuf[:, 0, :], abuf[:, 1, :])
        rows_p = jnp.where(low, abuf[:, 2, :], abuf[:, 3, :])
        at_full[...] = jnp.concatenate([rows_q, rows_p], axis=0).T.astype(BF16)
        mine = pl.ds(pl.multiple_of(lax.rem(i, 2) * 64, 64), 64)
        at_buf[...] = at_full[mine, :]

        @pl.loop(0, FS - 1)
        def _(t):
            send(at_full.at[mine], at_buf, RELAY, (i, fs_index(t)))

    arrived(bbuf.at[pl.ds(0, DP - 1)], BANK)
    bank_e = jnp.concatenate([bbuf[:, 0, :], bbuf[:, 1, :]], axis=1).astype(BF16)
    bank_o = jnp.concatenate([bbuf[:, 2, :], bbuf[:, 3, :]], axis=1).astype(BF16)
    g = gain_v[:, own]

    arrived(nbuf.at[pl.ds(0, DP - 1)], NORM)
    nq = jnp.concatenate([nbuf[:, 0, :], nbuf[:, 1, :]], axis=1)
    np_ = jnp.concatenate([nbuf[:, 2, :], nbuf[:, 3, :]], axis=1)
    eq = (nq * g).astype(BF16)
    ep = (np_ * g).astype(BF16)
    right = jnp.concatenate([ep, bank_e, bank_o], axis=0)
    st = dot(right, eq, 1, 1)
    bank_st = st[64:192]
    flat[0:32, 0:64] = st[0:32]
    flat[0:32, 64:128] = st[32:64]
    flat[32:40, :] = jnp.zeros((8, 128), F32)
    for h in range(8):
        hit = jnp.where(bank_row == spot[h:h + 1], bank_st, 0.0)
        flat[32 + h:33 + h, 0:64] = jnp.sum(hit, axis=0, keepdims=True)
    for k in range(10):
        pay[k // 5, k % 5] = flat[4 * k:4 * k + 4]
    send(pay.at[1 - c], cb4, SPAIR, partner)
    arrived(cb4, SPAIR)
    half4[...] = pay[c] + cb4[...]
    yb4[y] = half4[...]

    @pl.loop(0, SIDE - 1)
    def _(t):
        send(half4, yb4.at[y], SY, y_peer(t))

    arrived(yb4.at[pl.ds(0, SIDE - 1)], SY)
    tot[c] = jnp.sum(yb4[...], axis=0)
    send(tot.at[c], tot.at[c], SBACK, partner)
    arrived(tot.at[0], SBACK)
    for k in range(10):
        flat[4 * k:4 * k + 4] = tot[k // 5, k % 5]
    scores = jnp.concatenate([flat[0:32, 0:64], flat[0:32, 64:128]], axis=0) * SCALE
    hard = flat[32:40, 0:64] * SCALE

    top = jnp.maximum(jnp.max(scores, axis=0, keepdims=True), jnp.max(hard, axis=0, keepdims=True))
    row_lse = top + jnp.log(
        jnp.sum(jnp.exp(scores - top), axis=0, keepdims=True)
        + jnp.sum(jnp.exp(hard - top), axis=0, keepdims=True)
    )
    peak = jnp.max(scores, axis=1, keepdims=True)
    col_lse = peak + jnp.log(jnp.sum(jnp.exp(scores - peak), axis=1, keepdims=True))
    diag = jnp.sum(jnp.where(eye, scores, 0.0), axis=1, keepdims=True)
    loss_out[...] = (
        jnp.sum(row_lse, axis=1, keepdims=True)
        + jnp.sum(col_lse - 2.0 * diag, axis=0, keepdims=True)
    ) * (1.0 / COUNT)
    dscore = (jnp.exp(scores - row_lse) + jnp.exp(scores - col_lse) - 2.0 * eye_f) * (1.0 / COUNT)
    dhard = jnp.exp(hard - row_lse) * (1.0 / COUNT)
    weight = jnp.zeros((128, 64), F32)
    for h in range(8):
        weight = weight + jnp.where(bank_row == spot[h:h + 1], dhard[h:h + 1], 0.0)
    weighted = dscore * scores
    centre_p = jnp.sum(weighted, axis=1, keepdims=True) * (1.0 / D)
    centre_row = (
        jnp.sum(weighted, axis=0, keepdims=True) + jnp.sum(dhard * hard, axis=0, keepdims=True)
    ) * (1.0 / D)
    centre_q = jnp.sum(jnp.where(eye, centre_row, 0.0), axis=1, keepdims=True)

    gq = dot2(jnp.concatenate([dscore, weight], axis=0), right, 0, 0) * (g * SCALE)
    gp = dot2(dscore, eq, 1, 0) * (g * SCALE)
    arrived(ibuf.at[pl.ds(0, DP - 1)], INV)
    inv = ibuf[:, 0, :]
    hq = inv[:, 0:1] * (gq - nq * centre_q)
    hp = inv[:, 64:65] * (gp - np_ * centre_p)
    gh = jnp.concatenate([hq, hp], axis=0)

    @pl.when(relay != j)
    def _():
        arrived(at_buf, RELAY)

    at = at_buf[...]
    gh_hi = gh.astype(BF16)
    gh_lo = (gh - gh_hi.astype(F32)).astype(BF16)
    grad_out[...] = dot(at, gh_hi, 1, 0) + dot(at, gh_lo, 1, 0)

    sent(rcv1.at[0, pl.ds(0, FS - 1)], ATTN)
    sent(rcv1.at[1, pl.ds(0, FS - 1)], RESID)
    sent(bbuf.at[pl.ds(0, DP - 1)], BANK)
    sent(cbuf, PAIR)
    sent(ybuf.at[pl.ds(0, SIDE - 1)], YSUM)
    sent(sq, SQ)
    sent(nbuf.at[pl.ds(0, DP - 1)], NORM)
    sent(ibuf.at[pl.ds(0, DP - 1)], INV)
    sent(cb4, SPAIR)
    sent(yb4.at[pl.ds(0, SIDE - 1)], SY)
    sent(tot.at[0], SBACK)

    @pl.loop(0, 4)
    def _(t):
        @pl.when(4 * j + t != i)
        def _():
            sent(asrc, COLS)

    @pl.when(relay == j)
    def _():
        @pl.loop(0, FS - 1)
        def _(t):
            sent(at_buf, RELAY)


def on_device(attn, resid, lengths, out_proj, norm_gain, bank, hard_ids):
    any_spec = pl.BlockSpec(memory_space=pl.ANY)
    vmem = pltpu.VMEM
    loss, grad = pl.pallas_call(
        kernel,
        name="infonce",
        out_shape=(
            jax.ShapeDtypeStruct((1, 1), F32),
            jax.ShapeDtypeStruct((64, BLK), F32),
        ),
        in_specs=[any_spec] * 7,
        out_specs=(pl.BlockSpec(memory_space=vmem), pl.BlockSpec(memory_space=vmem)),
        scratch_shapes=[
            vmem((2, 64, D), BF16),
            vmem((2, 64, D), BF16),
            pltpu.SMEM((1, 2), jnp.int32),
            vmem((BLK, D), BF16),
            vmem((1, D), F32),
            vmem((2, D), BF16),
            vmem((8, 64), jnp.int32),
            vmem((2, FS, 4, 128), F32),
            vmem((2, FS, 4, 128), F32),
            vmem((16, BLK), F32),
            vmem((2, SIDE, 4, 128), F32),
            vmem((SIDE, 4, 128), F32),
            vmem((SIDE, 4, 128), F32),
            vmem((SIDE, SIDE, 4, 128), F32),
            vmem((SIDE, 4, 128), F32),
            vmem((4, 128), F32),
            vmem((4, 128), F32),
            vmem((4, 128), F32),
            vmem((DP, 4, 128), F32),
            vmem((1, 128), F32),
            vmem((DP, 1, 128), F32),
            vmem((4, 128), F32),
            vmem((DP, 4, 128), F32),
            vmem((4, 128), F32),
            vmem((DP, 4, 128), F32),
            vmem((128, 128), BF16),
            vmem((64, 128), BF16),
            vmem((2, 5, 4, 128), F32),
            vmem((5, 4, 128), F32),
            vmem((5, 4, 128), F32),
            vmem((SIDE, 5, 4, 128), F32),
            vmem((2, 5, 4, 128), F32),
            vmem((40, 128), F32),
            pltpu.SemaphoreType.DMA((7,)),
            pltpu.SemaphoreType.DMA((KINDS,)),
            pltpu.SemaphoreType.DMA((KINDS,)),
        ],
        compiler_params=pltpu.CompilerParams(
            collective_id=0, has_side_effects=True, vmem_limit_bytes=62 * 2**20
        ),
        cost_estimate=pl.CostEstimate(flops=10**8, bytes_accessed=4 * 2**20, transcendentals=10**4),
    )(attn, resid, lengths, out_proj, norm_gain.reshape(1, D), bank, hard_ids.T)
    return (loss[0, 0], grad)


def solution(mesh):
    placed = (
        P("dp", None, "fsdp", None),
        P("dp", None, "fsdp", None),
        P("dp", None),
        P("fsdp", None),
        P(),
        P("dp", None),
        P(),
    )
    return jax.shard_map(
        on_device, mesh=mesh, in_specs=placed, out_specs=(P(), P("dp", "fsdp")), check_vma=False
    )
```

```python
import jax
import jax.numpy as jnp
from jax import lax
from jax.experimental import pallas as pl
from jax.experimental.pallas import tpu as pltpu
from jax.sharding import PartitionSpec as P

MESH = pl.DeviceIdType.MESH
F32 = jnp.float32
BF16 = jnp.bfloat16

SIDE = 8
DP = 64
FS = 16
D = 4096
BLK = 256
SCALE = 4.0 / 64.0
COUNT = 128.0

ATTN, RESID, BANK, COLS, PAIR, YSUM, YOWN, SQ, NORM, REST, INV, RELAY, SPAIR, SY, SBACK = range(15)
KINDS = 15


FAR = (4, 5, 3, 6, 2, 7, 1, 0)


def far(m):
    return lax.rem(12 + (2 * lax.rem(m, 2) - 1) * lax.div(m + 1, 2), SIDE)


def dot(a, b, ca, cb):
    return lax.dot_general(a, b, (((ca,), (cb,)), ((), ())), preferred_element_type=F32)


def dot2(a, b, ca, cb):
    hi = a.astype(BF16)
    lo = (a - hi.astype(F32)).astype(BF16)
    return dot(hi, b, ca, cb) + dot(lo, b, ca, cb)


def kernel(
    attn, resid, lengths, w, gain, bank, ids, loss_out, grad_out,
    attn_v, resid_v, len_s, w_v, gain_v, bank_v, ids_v,
    src1, rcv1, lhs, part, cbuf, half, half_b, ybuf, yown, sq, sqr,
    nsrc, nbuf, isrc, ibuf, bsrc, bbuf, asrc, abuf, at_full, at_buf,
    pay, cb4, half4, yb4, tot, flat, rsrc, rbuf, quad, wide, local_sem, ssem, rsem, plane,
):
    i = lax.axis_index("dp")
    j = lax.axis_index("fsdp")
    x, z = lax.div(i, SIDE), lax.rem(i, SIDE)
    y, c = lax.div(j, 2), lax.rem(j, 2)
    partner = (i, 2 * y + 1 - c)

    pz = [lax.rem(z + m, SIDE) for m in FAR]
    py = [2 * lax.rem(y + m, SIDE) for m in FAR]

    def each_dp(act):
        @pl.loop(0, SIDE - 1)
        def _(t):
            px = lax.rem(x + far(t), SIDE) * SIDE
            for b in range(SIDE):
                act((px + pz[b], j))

        for b in range(SIDE - 1):
            act((x * SIDE + pz[b], j))

    def each_fs(act):
        for b in range(SIDE - 1):
            act(py[b] + 1 - c)
            act(py[b] + c)
        act(2 * y + 1 - c)

    def each_y(act):
        for b in range(SIDE - 1):
            act((i, py[b] + c))

    def send(src, dst, kind, to):
        pltpu.make_async_remote_copy(
            src_ref=src, dst_ref=dst, send_sem=ssem.at[kind], recv_sem=rsem.at[kind],
            device_id=to, device_id_type=MESH,
        ).start()

    def arrived(ref, kind):
        pltpu.make_async_copy(ref, ref, rsem.at[kind]).wait()

    def sent(ref, kind):
        pltpu.make_async_copy(ref, ref, ssem.at[kind]).wait()

    def rows_of(buf):
        wide[...] = buf[...].astype(F32)
        return (
            jnp.concatenate([wide[:, 0, :], wide[:, 1, :]], axis=1),
            jnp.concatenate([wide[:, 2, :], wide[:, 3, :]], axis=1),
        )

    loads = [
        pltpu.make_async_copy(a, b, local_sem.at[n])
        for n, (a, b) in enumerate([
            (lengths, len_s), (attn.at[0], attn_v), (resid.at[0], resid_v), (bank, bank_v),
            (ids, ids_v), (gain, gain_v), (w, w_v),
        ])
    ]
    for load in loads:
        load.start()

    barrier = pltpu.get_barrier_semaphore()

    def greet(to):
        pl.semaphore_signal(barrier, inc=1, device_id=to, device_id_type=MESH)

    px = [lax.rem(x + m, SIDE) * SIDE for m in FAR]

    each_fs(lambda to: greet((i, to)))
    for b in range(SIDE - 1):
        greet((x * SIDE + pz[b], j))
        greet((px[b] + z, j))

    loads[0].wait()
    loads[1].wait()
    row = lax.broadcasted_iota(jnp.int32, (16, 128), 0)
    col = lax.broadcasted_iota(jnp.int32, (16, 128), 1)
    place_q = len_s[0, 0] - 1 - 64 * j
    place_p = len_s[0, 1] - 1 - 64 * j
    pick = jnp.where(
        row < 2,
        jnp.where(col < 64, col, -1) - place_q,
        jnp.where(col >= 64, col - 64, -1) - place_p,
    )
    inside = jnp.where(row < 2, jnp.where(col < 64, 1, 0), jnp.where(col >= 64, 1, 0))
    select = jnp.where((pick == 0) & (inside == 1), 1.0, 0.0).astype(BF16)
    even = lax.rem(row, 2) == 0

    def fold(block):
        return jnp.where(even, block[:, :128], block[:, 128:])[0:4]

    for t in range(FS):
        src1[0, t] = fold(dot(select, attn_v[:, :, t * BLK:(t + 1) * BLK].reshape(128, BLK), 1, 0)).astype(BF16)
    rcv1[0, j] = src1[0, j]
    pl.semaphore_wait(barrier, FS - 1 + 2 * (SIDE - 1))

    each_fs(lambda to: send(src1.at[0, to], rcv1.at[0, j], ATTN, (i, to)))

    for b in range(SIDE - 1):
        pl.semaphore_signal(plane, inc=1, device_id=(px[b] + z, j), device_id_type=MESH)
    loads[2].wait()
    for t in range(FS):
        src1[1, t] = fold(dot(select, resid_v[:, :, t * BLK:(t + 1) * BLK].reshape(128, BLK), 1, 0)).astype(BF16)
    rcv1[1, j] = src1[1, j]

    each_fs(lambda to: send(src1.at[1, to], rcv1.at[1, j], RESID, (i, to)))

    loads[3].wait()
    own = pl.ds(pl.multiple_of(j * BLK, BLK), BLK)
    bank_rows = bank_v[:, own].astype(F32)
    for r in range(4):
        quad[r:r + 1] = bank_rows[r // 2:r // 2 + 1, 128 * (r % 2):128 * (r % 2) + 128]
    bsrc[...] = quad[...].astype(BF16)
    bbuf[i] = bsrc[...]

    lhs[...] = jnp.zeros_like(lhs)
    loads[6].wait()

    arrived(rcv1.at[0, pl.ds(0, FS - 1)], ATTN)
    block = jnp.sum(rcv1[0].astype(F32), axis=0)
    asrc[...] = block.astype(BF16)
    for r in range(4):
        lhs[r:r + 1, 0:128] = block[r - r % 2:r - r % 2 + 1]
        lhs[r:r + 1, 128:256] = block[r - r % 2 + 1:r - r % 2 + 2]
    rows = lhs[...].astype(BF16)
    for t in range(FS):
        part[t % 2, t // 2] = fold(dot(rows, w_v[:, t * BLK:(t + 1) * BLK], 1, 0))
    arrived(rcv1.at[1, pl.ds(0, FS - 1)], RESID)
    part[c, y] = part[c, y] + jnp.sum(rcv1[1].astype(F32), axis=0)
    send(part.at[1 - c], cbuf, PAIR, partner)

    arrived(cbuf, PAIR)
    half[...] = part[c] + cbuf[...]
    half_b[...] = half[...].astype(BF16)
    ybuf[y] = half_b[...]
    yown[y] = half[y]

    each_y(lambda to: send(half_b, ybuf.at[y], YSUM, to))
    for b in range(SIDE - 1):
        send(half.at[lax.div(py[b], 2)], yown.at[y], YOWN, (i, py[b] + c))
    pl.semaphore_wait(plane, SIDE - 1)

    @pl.loop(0, 4)
    def _(t):
        to = 4 * j + t

        @pl.when(to != i)
        def _():
            send(asrc, abuf.at[i], COLS, (to, j))

    relay = lax.div(i, 4)

    @pl.when(relay == j)
    def _():
        abuf[i] = asrc[...]

    each_dp(lambda to: send(bsrc, bbuf.at[i], BANK, to))

    loads[4].wait()
    loads[5].wait()
    eye = lax.broadcasted_iota(jnp.int32, (64, 64), 0) == lax.broadcasted_iota(jnp.int32, (64, 64), 1)
    eye_f = jnp.where(eye, 1.0, 0.0)
    ids_t = ids_v[...]
    spot = lax.rem(ids_t, 2) * 64 + lax.div(ids_t, 2)
    bank_row = lax.broadcasted_iota(jnp.int32, (128, 64), 0)

    arrived(ybuf.at[pl.ds(0, SIDE - 1)], YSUM)
    hid = jnp.sum(ybuf[...].astype(F32), axis=0)
    sq[...] = jnp.sum(hid * hid, axis=0)
    send(sq, sqr, SQ, partner)
    arrived(yown.at[pl.ds(0, SIDE - 1)], YOWN)
    own_hid = jnp.sum(yown[...], axis=0)
    arrived(sqr, SQ)
    sums = jnp.sum(sq[...] + sqr[...], axis=1, keepdims=True)
    inv_q = lax.rsqrt((sums[0:1] + sums[1:2]) * (1.0 / D) + 1e-5)
    inv_p = lax.rsqrt((sums[2:3] + sums[3:4]) * (1.0 / D) + 1e-5)
    four = lax.broadcasted_iota(jnp.int32, (4, 128), 0)
    g = gain_v[:, own]
    scaled = (own_hid * jnp.where(four < 2, inv_q, inv_p)) * jnp.where(
        lax.rem(four, 2) == 0, g[:, :128], g[:, 128:]
    )
    rounded = scaled.astype(BF16)
    nsrc[...] = rounded
    rsrc[...] = (scaled - rounded.astype(F32)).astype(BF16)
    lane = lax.broadcasted_iota(jnp.int32, (1, 128), 1)
    isrc[...] = jnp.where(lane < 64, inv_q, inv_p)

    each_dp(lambda to: send(nsrc, nbuf.at[i], NORM, to))

    nbuf[i] = nsrc[...]
    rbuf[i] = rsrc[...]
    ibuf[i] = isrc[...]

    each_dp(lambda to: send(rsrc, rbuf.at[i], REST, to))
    each_dp(lambda to: send(isrc, ibuf.at[i], INV, to))

    @pl.when(relay == j)
    def _():
        arrived(abuf.at[pl.ds(0, DP - 1)], COLS)
        low = lax.rem(i, 4) < 2
        wide[...] = abuf[...].astype(F32)
        rows_q = jnp.where(low, wide[:, 0, :], wide[:, 1, :])
        rows_p = jnp.where(low, wide[:, 2, :], wide[:, 3, :])
        at_full[...] = jnp.concatenate([rows_q, rows_p], axis=0).T.astype(BF16)
        mine = pl.ds(pl.multiple_of(lax.rem(i, 2) * 64, 64), 64)
        at_buf[...] = at_full[mine, :]

        each_fs(lambda to: send(at_full.at[mine], at_buf, RELAY, (i, to)))

    arrived(bbuf.at[pl.ds(0, DP - 1)], BANK)
    first_bank, second_bank = rows_of(bbuf)
    bank_e, bank_o = first_bank.astype(BF16), second_bank.astype(BF16)

    arrived(nbuf.at[pl.ds(0, DP - 1)], NORM)
    emb_q, emb_p = rows_of(nbuf)
    eq, ep = emb_q.astype(BF16), emb_p.astype(BF16)
    right = jnp.concatenate([ep, bank_e, bank_o], axis=0)
    st = dot(right, eq, 1, 1)
    bank_st = st[64:192]
    flat[0:32, 0:64] = st[0:32]
    flat[0:32, 64:128] = st[32:64]
    flat[32:40, :] = jnp.zeros((8, 128), F32)
    for h in range(8):
        hit = jnp.where(bank_row == spot[h:h + 1], bank_st, 0.0)
        flat[32 + h:33 + h, 0:64] = jnp.sum(hit, axis=0, keepdims=True)
    for k in range(10):
        pay[k // 5, k % 5] = flat[4 * k:4 * k + 4]
    send(pay.at[1 - c], cb4, SPAIR, partner)
    arrived(cb4, SPAIR)
    half4[...] = pay[c] + cb4[...]
    yb4[y] = half4[...]

    each_y(lambda to: send(half4, yb4.at[y], SY, to))

    arrived(rbuf.at[pl.ds(0, DP - 1)], REST)
    rest_q, rest_p = rows_of(rbuf)
    inv_g = 1.0 / g
    nq = (emb_q + rest_q) * inv_g
    np_ = (emb_p + rest_p) * inv_g
    arrived(ibuf.at[pl.ds(0, DP - 1)], INV)
    inv = ibuf[:, 0, :]
    @pl.when(relay != j)
    def _():
        arrived(at_buf, RELAY)

    arrived(yb4.at[pl.ds(0, SIDE - 1)], SY)
    tot[c] = jnp.sum(yb4[...], axis=0)
    send(tot.at[c], tot.at[c], SBACK, partner)
    arrived(tot.at[0], SBACK)
    for k in range(10):
        flat[4 * k:4 * k + 4] = tot[k // 5, k % 5]
    scores = jnp.concatenate([flat[0:32, 0:64], flat[0:32, 64:128]], axis=0) * SCALE
    hard = flat[32:40, 0:64] * SCALE

    top = jnp.maximum(jnp.max(scores, axis=0, keepdims=True), jnp.max(hard, axis=0, keepdims=True))
    row_lse = top + jnp.log(
        jnp.sum(jnp.exp(scores - top), axis=0, keepdims=True)
        + jnp.sum(jnp.exp(hard - top), axis=0, keepdims=True)
    )
    peak = jnp.max(scores, axis=1, keepdims=True)
    col_lse = peak + jnp.log(jnp.sum(jnp.exp(scores - peak), axis=1, keepdims=True))
    diag = jnp.sum(jnp.where(eye, scores, 0.0), axis=1, keepdims=True)
    loss_out[...] = (
        jnp.sum(row_lse, axis=1, keepdims=True)
        + jnp.sum(col_lse - 2.0 * diag, axis=0, keepdims=True)
    ) * (1.0 / COUNT)
    dscore = (jnp.exp(scores - row_lse) + jnp.exp(scores - col_lse) - 2.0 * eye_f) * (1.0 / COUNT)
    dhard = jnp.exp(hard - row_lse) * (1.0 / COUNT)
    weight = jnp.zeros((128, 64), F32)
    for h in range(8):
        weight = weight + jnp.where(bank_row == spot[h:h + 1], dhard[h:h + 1], 0.0)
    weighted = dscore * scores
    centre_p = jnp.sum(weighted, axis=1, keepdims=True) * (1.0 / D)
    centre_row = (
        jnp.sum(weighted, axis=0, keepdims=True) + jnp.sum(dhard * hard, axis=0, keepdims=True)
    ) * (1.0 / D)
    centre_q = jnp.sum(jnp.where(eye, centre_row, 0.0), axis=1, keepdims=True)

    gq = dot2(jnp.concatenate([dscore, weight], axis=0), right, 0, 0) * (g * SCALE)
    gp = dot2(dscore, eq, 1, 0) * (g * SCALE)
    hq = inv[:, 0:1] * (gq - nq * centre_q)
    hp = inv[:, 64:65] * (gp - np_ * centre_p)
    gh = jnp.concatenate([hq, hp], axis=0)
    at = at_buf[...]
    gh_hi = gh.astype(BF16)
    gh_lo = (gh - gh_hi.astype(F32)).astype(BF16)
    grad_out[...] = dot(at, gh_hi, 1, 0) + dot(at, gh_lo, 1, 0)

    sent(rcv1.at[0, pl.ds(0, FS - 1)], ATTN)
    sent(rcv1.at[1, pl.ds(0, FS - 1)], RESID)
    sent(bbuf.at[pl.ds(0, DP - 1)], BANK)
    sent(cbuf, PAIR)
    sent(ybuf.at[pl.ds(0, SIDE - 1)], YSUM)
    sent(yown.at[pl.ds(0, SIDE - 1)], YOWN)
    sent(sq, SQ)
    sent(nbuf.at[pl.ds(0, DP - 1)], NORM)
    sent(rbuf.at[pl.ds(0, DP - 1)], REST)
    sent(ibuf.at[pl.ds(0, DP - 1)], INV)
    sent(cb4, SPAIR)
    sent(yb4.at[pl.ds(0, SIDE - 1)], SY)
    sent(tot.at[0], SBACK)

    @pl.loop(0, 4)
    def _(t):
        @pl.when(4 * j + t != i)
        def _():
            sent(asrc, COLS)

    @pl.when(relay == j)
    def _():
        @pl.loop(0, FS - 1)
        def _(t):
            sent(at_buf, RELAY)


def on_device(attn, resid, lengths, out_proj, norm_gain, bank, hard_ids):
    any_spec = pl.BlockSpec(memory_space=pl.ANY)
    vmem = pltpu.VMEM
    loss, grad = pl.pallas_call(
        kernel,
        name="infonce",
        out_shape=(
            jax.ShapeDtypeStruct((1, 1), F32),
            jax.ShapeDtypeStruct((64, BLK), F32),
        ),
        in_specs=[any_spec] * 7,
        out_specs=(pl.BlockSpec(memory_space=vmem), pl.BlockSpec(memory_space=vmem)),
        scratch_shapes=[
            vmem((2, 64, D), BF16),
            vmem((2, 64, D), BF16),
            pltpu.SMEM((1, 2), jnp.int32),
            vmem((BLK, D), BF16),
            vmem((1, D), F32),
            vmem((2, D), BF16),
            vmem((8, 64), jnp.int32),
            vmem((2, FS, 4, 128), BF16),
            vmem((2, FS, 4, 128), BF16),
            vmem((16, BLK), F32),
            vmem((2, SIDE, 4, 128), F32),
            vmem((SIDE, 4, 128), F32),
            vmem((SIDE, 4, 128), F32),
            vmem((SIDE, 4, 128), BF16),
            vmem((SIDE, SIDE, 4, 128), BF16),
            vmem((SIDE, 4, 128), F32),
            vmem((4, 128), F32),
            vmem((4, 128), F32),
            vmem((4, 128), BF16),
            vmem((DP, 4, 128), BF16),
            vmem((1, 128), F32),
            vmem((DP, 1, 128), F32),
            vmem((4, 128), BF16),
            vmem((DP, 4, 128), BF16),
            vmem((4, 128), BF16),
            vmem((DP, 4, 128), BF16),
            vmem((128, 128), BF16),
            vmem((64, 128), BF16),
            vmem((2, 5, 4, 128), F32),
            vmem((5, 4, 128), F32),
            vmem((5, 4, 128), F32),
            vmem((SIDE, 5, 4, 128), F32),
            vmem((2, 5, 4, 128), F32),
            vmem((40, 128), F32),
            vmem((4, 128), BF16),
            vmem((DP, 4, 128), BF16),
            vmem((4, 128), F32),
            vmem((DP, 4, 128), F32),
            pltpu.SemaphoreType.DMA((7,)),
            pltpu.SemaphoreType.DMA((KINDS,)),
            pltpu.SemaphoreType.DMA((KINDS,)),
            pltpu.SemaphoreType.REGULAR,
        ],
        compiler_params=pltpu.CompilerParams(
            collective_id=0, has_side_effects=True, vmem_limit_bytes=62 * 2**20
        ),
        cost_estimate=pl.CostEstimate(flops=10**8, bytes_accessed=4 * 2**20, transcendentals=10**4),
    )(attn, resid, lengths, out_proj, norm_gain.reshape(1, D), bank, hard_ids.T)
    return (loss[0, 0], grad)


def solution(mesh):
    placed = (
        P("dp", None, "fsdp", None),
        P("dp", None, "fsdp", None),
        P("dp", None),
        P("fsdp", None),
        P(),
        P("dp", None),
        P(),
    )
    return jax.shard_map(
        on_device, mesh=mesh, in_specs=placed, out_specs=(P(), P("dp", "fsdp")), check_vma=False
    )
```

```python
import jax
import jax.numpy as jnp
from jax import lax
from jax.experimental import pallas as pl
from jax.experimental.pallas import tpu as pltpu
from jax.sharding import PartitionSpec as P

MESH = pl.DeviceIdType.MESH
F32 = jnp.float32
BF16 = jnp.bfloat16

SIDE = 8
DP = 64
FS = 16
D = 4096
BLK = 256
SCALE = 4.0 / 64.0
COUNT = 128.0

ATTN, RESID, BANK, COLS, WEIGHT, YSUM, YOWN, SQ, NORM, REST, INV, RELAY, SPAIR, SY, SBACK = range(15)
KINDS = 15


FAR = (4, 5, 3, 6, 2, 7, 1, 0)


def far(m):
    return lax.rem(12 + (2 * lax.rem(m, 2) - 1) * lax.div(m + 1, 2), SIDE)


def dot(a, b, ca, cb):
    return lax.dot_general(a, b, (((ca,), (cb,)), ((), ())), preferred_element_type=F32)


def dot2(a, b, ca, cb):
    hi = a.astype(BF16)
    lo = (a - hi.astype(F32)).astype(BF16)
    return dot(hi, b, ca, cb) + dot(lo, b, ca, cb)


def kernel(
    attn, resid, lengths, w, gain, bank, ids, loss_out, grad_out,
    attn_v, resid_v, len_s, w_v, gain_v, bank_v, ids_v,
    src_a, rcv_a, src_r, rcv_r, pooled, lhs, half, half_b, ybuf, yown, sq, sqr,
    nsrc, nbuf, isrc, ibuf, bsrc, bbuf, asrc, abuf, at_full, at_buf,
    pay, cb4, half4, yb4, tot, flat, rsrc, rbuf, quad, wide, local_sem, w_sem, ssem, rsem, plane,
):
    i = lax.axis_index("dp")
    j = lax.axis_index("fsdp")
    x, z = lax.div(i, SIDE), lax.rem(i, SIDE)
    y, c = lax.div(j, 2), lax.rem(j, 2)
    partner = (i, 2 * y + 1 - c)

    pz = [lax.rem(z + m, SIDE) for m in FAR]
    py = [2 * lax.rem(y + m, SIDE) for m in FAR]

    def each_dp(act):
        @pl.loop(0, SIDE - 1)
        def _(t):
            px = lax.rem(x + far(t), SIDE) * SIDE
            for b in range(SIDE):
                act((px + pz[b], j))

        for b in range(SIDE - 1):
            act((x * SIDE + pz[b], j))

    def each_fs(act):
        for b in range(SIDE - 1):
            act(py[b] + 1 - c)
            act(py[b] + c)
        act(2 * y + 1 - c)

    def each_y(act):
        for b in range(SIDE - 1):
            act((i, py[b] + c))

    def send(src, dst, kind, to):
        pltpu.make_async_remote_copy(
            src_ref=src, dst_ref=dst, send_sem=ssem.at[kind], recv_sem=rsem.at[kind],
            device_id=to, device_id_type=MESH,
        ).start()

    def arrived(ref, kind):
        pltpu.make_async_copy(ref, ref, rsem.at[kind]).wait()

    def sent(ref, kind):
        pltpu.make_async_copy(ref, ref, ssem.at[kind]).wait()

    def rows_of(buf):
        wide[...] = buf[...].astype(F32)
        return (
            jnp.concatenate([wide[:, 0, :], wide[:, 1, :]], axis=1),
            jnp.concatenate([wide[:, 2, :], wide[:, 3, :]], axis=1),
        )

    loads = [
        pltpu.make_async_copy(a, b, local_sem.at[n])
        for n, (a, b) in enumerate([
            (lengths, len_s), (attn.at[0], attn_v), (resid.at[0], resid_v), (bank, bank_v),
            (ids, ids_v), (gain, gain_v),
        ])
    ]

    def w_block(k, parity):
        return w.at[:, pl.ds(pl.multiple_of((2 * k + parity) * BLK, BLK), BLK)]

    own_w = [
        pltpu.make_async_copy(w_block(k, c), w_v.at[c, k], w_sem.at[k]) for k in range(SIDE)
    ]
    barrier = pltpu.get_barrier_semaphore()

    def greet(to):
        pl.semaphore_signal(barrier, inc=1, device_id=to, device_id_type=MESH)

    px = [lax.rem(x + m, SIDE) * SIDE for m in FAR]

    each_fs(lambda to: greet((i, to)))
    for load in loads[:2]:
        load.start()
    for b in range(SIDE - 1):
        greet((x * SIDE + pz[b], j))
        greet((px[b] + z, j))
    for load in loads[2:] + own_w:
        load.start()

    loads[0].wait()
    loads[1].wait()
    row = lax.broadcasted_iota(jnp.int32, (16, 128), 0)
    col = lax.broadcasted_iota(jnp.int32, (16, 128), 1)
    place_q = len_s[0, 0] - 1 - 64 * j
    place_p = len_s[0, 1] - 1 - 64 * j
    pick = jnp.where(
        row < 2,
        jnp.where(col < 64, col, -1) - place_q,
        jnp.where(col >= 64, col - 64, -1) - place_p,
    )
    inside = jnp.where(row < 2, jnp.where(col < 64, 1, 0), jnp.where(col >= 64, 1, 0))
    select = jnp.where((pick == 0) & (inside == 1), 1.0, 0.0).astype(BF16)
    even = lax.rem(row, 2) == 0

    def fold(block):
        return jnp.where(even, block[:, :128], block[:, 128:])[0:4]

    for t in range(FS):
        src_a[t // 2, t % 2] = fold(
            dot(select, attn_v[:, :, t * BLK:(t + 1) * BLK].reshape(128, BLK), 1, 0)
        ).astype(BF16)
    rcv_a[j] = src_a[y]
    pl.semaphore_wait(barrier, FS - 1 + 2 * (SIDE - 1))

    each_fs(lambda to: send(src_a.at[lax.div(to, 2)], rcv_a.at[j], ATTN, (i, to)))
    for k in range(SIDE):
        send(w_block(k, 1 - c), w_v.at[c, k], WEIGHT, partner)

    for b in range(SIDE - 1):
        pl.semaphore_signal(plane, inc=1, device_id=(px[b] + z, j), device_id_type=MESH)
    loads[2].wait()
    for t in range(FS):
        src_r[t] = fold(
            dot(select, resid_v[:, :, t * BLK:(t + 1) * BLK].reshape(128, BLK), 1, 0)
        ).astype(BF16)
    rcv_r[j] = src_r[j]

    each_fs(lambda to: send(src_r.at[to], rcv_r.at[j], RESID, (i, to)))

    loads[3].wait()
    own = pl.ds(pl.multiple_of(j * BLK, BLK), BLK)
    bank_rows = bank_v[:, own].astype(F32)
    for r in range(4):
        quad[r:r + 1] = bank_rows[r // 2:r // 2 + 1, 128 * (r % 2):128 * (r % 2) + 128]
    bsrc[...] = quad[...].astype(BF16)
    bbuf[i] = bsrc[...]

    lhs[...] = jnp.zeros_like(lhs)
    for load in own_w:
        load.wait()

    arrived(rcv_a.at[pl.ds(0, FS - 1)], ATTN)
    pooled[...] = jnp.sum(rcv_a[...].astype(F32), axis=0)
    for b in range(2):
        for r in range(4):
            pick_r = r - r % 2
            lhs[r:r + 1, BLK * b:BLK * b + 128] = pooled[b, pick_r:pick_r + 1]
            lhs[r:r + 1, BLK * b + 128:BLK * (b + 1)] = pooled[b, pick_r + 1:pick_r + 2]
    rows = lhs[...].astype(BF16)
    arrived(w_v.at[0], WEIGHT)
    for k in range(SIDE):
        half[k] = fold(dot(rows[:, :BLK], w_v[0, k], 1, 0) + dot(rows[:, BLK:], w_v[1, k], 1, 0))
    arrived(rcv_r.at[pl.ds(0, FS - 1)], RESID)
    half[y] = half[y] + jnp.sum(rcv_r[...].astype(F32), axis=0)
    half_b[...] = half[...].astype(BF16)
    ybuf[y] = half_b[...]
    yown[y] = half[y]

    each_y(lambda to: send(half_b, ybuf.at[y], YSUM, to))
    for b in range(SIDE - 1):
        send(half.at[lax.div(py[b], 2)], yown.at[y], YOWN, (i, py[b] + c))
    asrc[...] = pooled[c].astype(BF16)
    pl.semaphore_wait(plane, SIDE - 1)

    @pl.loop(0, 4)
    def _(t):
        to = 4 * j + t

        @pl.when(to != i)
        def _():
            send(asrc, abuf.at[i], COLS, (to, j))

    relay = lax.div(i, 4)

    @pl.when(relay == j)
    def _():
        abuf[i] = asrc[...]

    each_dp(lambda to: send(bsrc, bbuf.at[i], BANK, to))

    loads[4].wait()
    loads[5].wait()
    eye = lax.broadcasted_iota(jnp.int32, (64, 64), 0) == lax.broadcasted_iota(jnp.int32, (64, 64), 1)
    eye_f = jnp.where(eye, 1.0, 0.0)
    ids_t = ids_v[...]
    spot = lax.rem(ids_t, 2) * 64 + lax.div(ids_t, 2)
    bank_row = lax.broadcasted_iota(jnp.int32, (128, 64), 0)

    arrived(ybuf.at[pl.ds(0, SIDE - 1)], YSUM)
    hid = jnp.sum(ybuf[...].astype(F32), axis=0)
    sq[...] = jnp.sum(hid * hid, axis=0)
    send(sq, sqr, SQ, partner)
    arrived(yown.at[pl.ds(0, SIDE - 1)], YOWN)
    own_hid = jnp.sum(yown[...], axis=0)
    arrived(sqr, SQ)
    sums = jnp.sum(sq[...] + sqr[...], axis=1, keepdims=True)
    inv_q = lax.rsqrt((sums[0:1] + sums[1:2]) * (1.0 / D) + 1e-5)
    inv_p = lax.rsqrt((sums[2:3] + sums[3:4]) * (1.0 / D) + 1e-5)
    four = lax.broadcasted_iota(jnp.int32, (4, 128), 0)
    g = gain_v[:, own]
    scaled = (own_hid * jnp.where(four < 2, inv_q, inv_p)) * jnp.where(
        lax.rem(four, 2) == 0, g[:, :128], g[:, 128:]
    )
    rounded = scaled.astype(BF16)
    nsrc[...] = rounded
    rsrc[...] = (scaled - rounded.astype(F32)).astype(BF16)
    lane = lax.broadcasted_iota(jnp.int32, (1, 128), 1)
    isrc[...] = jnp.where(lane < 64, inv_q, inv_p)

    each_dp(lambda to: send(nsrc, nbuf.at[i], NORM, to))

    nbuf[i] = nsrc[...]
    rbuf[i] = rsrc[...]
    ibuf[i] = isrc[...]

    each_dp(lambda to: send(rsrc, rbuf.at[i], REST, to))
    each_dp(lambda to: send(isrc, ibuf.at[i], INV, to))

    @pl.when(relay == j)
    def _():
        arrived(abuf.at[pl.ds(0, DP - 1)], COLS)
        low = lax.rem(i, 4) < 2
        wide[...] = abuf[...].astype(F32)
        rows_q = jnp.where(low, wide[:, 0, :], wide[:, 1, :])
        rows_p = jnp.where(low, wide[:, 2, :], wide[:, 3, :])
        at_full[...] = jnp.concatenate([rows_q, rows_p], axis=0).T.astype(BF16)
        mine = pl.ds(pl.multiple_of(lax.rem(i, 2) * 64, 64), 64)
        at_buf[...] = at_full[mine, :]

        each_fs(lambda to: send(at_full.at[mine], at_buf, RELAY, (i, to)))

    arrived(bbuf.at[pl.ds(0, DP - 1)], BANK)
    first_bank, second_bank = rows_of(bbuf)
    bank_e, bank_o = first_bank.astype(BF16), second_bank.astype(BF16)

    arrived(nbuf.at[pl.ds(0, DP - 1)], NORM)
    emb_q, emb_p = rows_of(nbuf)
    eq, ep = emb_q.astype(BF16), emb_p.astype(BF16)
    right = jnp.concatenate([ep, bank_e, bank_o], axis=0)
    st = dot(right, eq, 1, 1)
    bank_st = st[64:192]
    flat[0:32, 0:64] = st[0:32]
    flat[0:32, 64:128] = st[32:64]
    flat[32:40, :] = jnp.zeros((8, 128), F32)
    for h in range(8):
        hit = jnp.where(bank_row == spot[h:h + 1], bank_st, 0.0)
        flat[32 + h:33 + h, 0:64] = jnp.sum(hit, axis=0, keepdims=True)
    for k in range(10):
        pay[k // 5, k % 5] = flat[4 * k:4 * k + 4]
    send(pay.at[1 - c], cb4, SPAIR, partner)
    arrived(cb4, SPAIR)
    half4[...] = pay[c] + cb4[...]
    yb4[y] = half4[...]

    each_y(lambda to: send(half4, yb4.at[y], SY, to))

    arrived(rbuf.at[pl.ds(0, DP - 1)], REST)
    rest_q, rest_p = rows_of(rbuf)
    inv_g = 1.0 / g
    nq = (emb_q + rest_q) * inv_g
    np_ = (emb_p + rest_p) * inv_g
    arrived(ibuf.at[pl.ds(0, DP - 1)], INV)
    inv = ibuf[:, 0, :]
    @pl.when(relay != j)
    def _():
        arrived(at_buf, RELAY)

    arrived(yb4.at[pl.ds(0, SIDE - 1)], SY)
    tot[c] = jnp.sum(yb4[...], axis=0)
    send(tot.at[c], tot.at[c], SBACK, partner)
    arrived(tot.at[0], SBACK)
    for k in range(10):
        flat[4 * k:4 * k + 4] = tot[k // 5, k % 5]
    scores = jnp.concatenate([flat[0:32, 0:64], flat[0:32, 64:128]], axis=0) * SCALE
    hard = flat[32:40, 0:64] * SCALE

    top = jnp.maximum(jnp.max(scores, axis=0, keepdims=True), jnp.max(hard, axis=0, keepdims=True))
    row_lse = top + jnp.log(
        jnp.sum(jnp.exp(scores - top), axis=0, keepdims=True)
        + jnp.sum(jnp.exp(hard - top), axis=0, keepdims=True)
    )
    peak = jnp.max(scores, axis=1, keepdims=True)
    col_lse = peak + jnp.log(jnp.sum(jnp.exp(scores - peak), axis=1, keepdims=True))
    diag = jnp.sum(jnp.where(eye, scores, 0.0), axis=1, keepdims=True)
    loss_out[...] = (
        jnp.sum(row_lse, axis=1, keepdims=True)
        + jnp.sum(col_lse - 2.0 * diag, axis=0, keepdims=True)
    ) * (1.0 / COUNT)
    dscore = (jnp.exp(scores - row_lse) + jnp.exp(scores - col_lse) - 2.0 * eye_f) * (1.0 / COUNT)
    dhard = jnp.exp(hard - row_lse) * (1.0 / COUNT)
    weight = jnp.zeros((128, 64), F32)
    for h in range(8):
        weight = weight + jnp.where(bank_row == spot[h:h + 1], dhard[h:h + 1], 0.0)
    weighted = dscore * scores
    centre_p = jnp.sum(weighted, axis=1, keepdims=True) * (1.0 / D)
    centre_row = (
        jnp.sum(weighted, axis=0, keepdims=True) + jnp.sum(dhard * hard, axis=0, keepdims=True)
    ) * (1.0 / D)
    centre_q = jnp.sum(jnp.where(eye, centre_row, 0.0), axis=1, keepdims=True)

    gq = dot2(jnp.concatenate([dscore, weight], axis=0), right, 0, 0) * (g * SCALE)
    gp = dot2(dscore, eq, 1, 0) * (g * SCALE)
    hq = inv[:, 0:1] * (gq - nq * centre_q)
    hp = inv[:, 64:65] * (gp - np_ * centre_p)
    gh = jnp.concatenate([hq, hp], axis=0)
    at = at_buf[...]
    gh_hi = gh.astype(BF16)
    gh_lo = (gh - gh_hi.astype(F32)).astype(BF16)
    grad_out[...] = dot(at, gh_hi, 1, 0) + dot(at, gh_lo, 1, 0)

    sent(rcv_a.at[pl.ds(0, FS - 1)], ATTN)
    sent(w_v.at[0], WEIGHT)
    sent(rcv_r.at[pl.ds(0, FS - 1)], RESID)
    sent(bbuf.at[pl.ds(0, DP - 1)], BANK)
    sent(ybuf.at[pl.ds(0, SIDE - 1)], YSUM)
    sent(yown.at[pl.ds(0, SIDE - 1)], YOWN)
    sent(sq, SQ)
    sent(nbuf.at[pl.ds(0, DP - 1)], NORM)
    sent(rbuf.at[pl.ds(0, DP - 1)], REST)
    sent(ibuf.at[pl.ds(0, DP - 1)], INV)
    sent(cb4, SPAIR)
    sent(yb4.at[pl.ds(0, SIDE - 1)], SY)
    sent(tot.at[0], SBACK)

    @pl.loop(0, 4)
    def _(t):
        @pl.when(4 * j + t != i)
        def _():
            sent(asrc, COLS)

    @pl.when(relay == j)
    def _():
        @pl.loop(0, FS - 1)
        def _(t):
            sent(at_buf, RELAY)


def on_device(attn, resid, lengths, out_proj, norm_gain, bank, hard_ids):
    any_spec = pl.BlockSpec(memory_space=pl.ANY)
    vmem = pltpu.VMEM
    loss, grad = pl.pallas_call(
        kernel,
        name="infonce",
        out_shape=(
            jax.ShapeDtypeStruct((1, 1), F32),
            jax.ShapeDtypeStruct((64, BLK), F32),
        ),
        in_specs=[any_spec] * 7,
        out_specs=(pl.BlockSpec(memory_space=vmem), pl.BlockSpec(memory_space=vmem)),
        scratch_shapes=[
            vmem((2, 64, D), BF16),
            vmem((2, 64, D), BF16),
            pltpu.SMEM((1, 2), jnp.int32),
            vmem((2, SIDE, BLK, BLK), BF16),
            vmem((1, D), F32),
            vmem((2, D), BF16),
            vmem((8, 64), jnp.int32),
            vmem((SIDE, 2, 4, 128), BF16),
            vmem((FS, 2, 4, 128), BF16),
            vmem((FS, 4, 128), BF16),
            vmem((FS, 4, 128), BF16),
            vmem((2, 4, 128), F32),
            vmem((16, 2 * BLK), F32),
            vmem((SIDE, 4, 128), F32),
            vmem((SIDE, 4, 128), BF16),
            vmem((SIDE, SIDE, 4, 128), BF16),
            vmem((SIDE, 4, 128), F32),
            vmem((4, 128), F32),
            vmem((4, 128), F32),
            vmem((4, 128), BF16),
            vmem((DP, 4, 128), BF16),
            vmem((1, 128), F32),
            vmem((DP, 1, 128), F32),
            vmem((4, 128), BF16),
            vmem((DP, 4, 128), BF16),
            vmem((4, 128), BF16),
            vmem((DP, 4, 128), BF16),
            vmem((128, 128), BF16),
            vmem((64, 128), BF16),
            vmem((2, 5, 4, 128), F32),
            vmem((5, 4, 128), F32),
            vmem((5, 4, 128), F32),
            vmem((SIDE, 5, 4, 128), F32),
            vmem((2, 5, 4, 128), F32),
            vmem((40, 128), F32),
            vmem((4, 128), BF16),
            vmem((DP, 4, 128), BF16),
            vmem((4, 128), F32),
            vmem((DP, 4, 128), F32),
            pltpu.SemaphoreType.DMA((6,)),
            pltpu.SemaphoreType.DMA((SIDE,)),
            pltpu.SemaphoreType.DMA((KINDS,)),
            pltpu.SemaphoreType.DMA((KINDS,)),
            pltpu.SemaphoreType.REGULAR,
        ],
        compiler_params=pltpu.CompilerParams(
            collective_id=0, has_side_effects=True, vmem_limit_bytes=62 * 2**20
        ),
        cost_estimate=pl.CostEstimate(flops=10**8, bytes_accessed=4 * 2**20, transcendentals=10**4),
    )(attn, resid, lengths, out_proj, norm_gain.reshape(1, D), bank, hard_ids.T)
    return (loss[0, 0], grad)


def solution(mesh):
    placed = (
        P("dp", None, "fsdp", None),
        P("dp", None, "fsdp", None),
        P("dp", None),
        P("fsdp", None),
        P(),
        P("dp", None),
        P(),
    )
    return jax.shard_map(
        on_device, mesh=mesh, in_specs=placed, out_specs=(P(), P("dp", "fsdp")), check_vma=False
    )
```
